32 devices in a mesh: ctx: 8 (over z, x), exp: 4 (over y, core).
Axes of the slice: x: 2, y: 2, z: 4, core: 2. Of those that a mesh axis runs over, the one named last changes fastest.
Arguments:
- stored: bfloat16 [4, 4096, 2048], P(None, 'ctx'), may hold values from -50 to 50
- depth_weights: float32 [4], replicated, may hold values from 0.2 to 1
- attn_gain: float32 [2048], replicated, may hold values from 0.5 to 1.5
- qkv_proj: bfloat16 [2048, 3, 16, 128], P(None, None, 'exp'), may hold values from -0.125 to 0.125
- q_gain: float32 [16, 128], P('exp'), may hold values from 1 to 2.5
- k_gain: float32 [16, 128], P('exp'), may hold values from 1 to 2.5
- out_proj: bfloat16 [2048, 2048], P('exp'), may hold values from -0.5 to 0.5
- moe_gain: float32 [2048], replicated, may hold values from 0.5 to 1.5
- router: bfloat16 [2048, 16], replicated, may hold values from -0.125 to 0.125
- gate_proj: bfloat16 [2048, 22528], P(None, ('ctx', 'exp')), may hold values from -0.125 to 0.125
- up_proj: bfloat16 [2048, 22528], P(None, ('ctx', 'exp')), may hold values from -0.125 to 0.125
- down_proj: bfloat16 [22528, 2048], P(('ctx', 'exp')), may hold values from -0.15625 to 0.15625
- expert_ids: int32 [4096, 6], P(('ctx', 'exp')), may hold values from 0 to 15, all different within a row; in each aligned block of 128 rows (0 to 127, 128 to 255, ...) at most 64 rows name the same one
- block_pattern: int32 [16, 64, 8], replicated, may hold values from -1 to 63, as said below
Outputs:
- layer_out: bfloat16 [4096, 2048], P(('ctx', 'exp'))
The draws below stay inside these ranges and needn't reach their ends.
Inputs may be any that keep to these rules, and one draw needn't show every extreme that they name: `expert_ids`: each row names 6 different experts; among the 128 rows of one device no expert is named by more than 64 rows, and some device reaches 64. Entry 0 of block_pattern[h, b] is b; the other 7 entries are distinct blocks before b, or -1 where fewer blocks precede b.
All inputs are finite; a program needn't handle non-finite values.
Results may differ from the reference program's by a relative error of at most 0.015.
Values may be sent and summed in bfloat16 or wider, within the bound.
A program may use at most 128 MiB of HBM per device.

```python
import math
import jax
import jax.numpy as jnp
import numpy as np
from jax import lax

D = 2048
HEADS = 16
DH = 128
FF = 1408
TOPK = 6
DEPTH = 4
BLK = 64
KL = 8
TOK = 128
EXPERTS = 16
SEQ = 4096
NB = 64
CAP = 64
N_CTX = 8
N_EXP = 4


def draw_stored(key, part):
    first, second, third = jax.random.split(key, 3)
    shape = (DEPTH, SEQ, D)
    row_scale = jnp.exp(jax.random.uniform(second, (DEPTH, SEQ, 1), jnp.float32, -1.15, 1.15))
    col_scale = jnp.exp(jax.random.uniform(third, (1, 1, D), jnp.float32, -1.15, 1.15))
    base = jnp.clip(jax.random.normal(first, shape, jnp.float32), -5.0, 5.0)
    return (base * row_scale * col_scale).astype(jnp.bfloat16)


def draw_block_pattern(key, part):
    shape = (HEADS, NB, NB)
    columns = lax.broadcasted_iota(jnp.int32, shape, 2)
    rows = lax.broadcasted_iota(jnp.int32, shape, 1)
    scores = jax.random.randint(key, shape, 0, 4096, jnp.int32) * NB + columns
    scores = jnp.where(columns < rows, scores, -1)
    top_vals, top_idx = lax.top_k(scores, KL - 1)
    picked = jnp.where(top_vals >= 0, top_idx, -1).astype(jnp.int32)
    own = lax.broadcasted_iota(jnp.int32, (HEADS, NB, 1), 1)
    return jnp.concatenate([own, picked], axis=2)


def block_levels(key, extent, pieces, smallest, top_value):
    gain = 1.0
    for dim, blocks in pieces:
        steps = jax.random.uniform(jax.random.fold_in(jax.random.fold_in(key, 6), dim), (blocks,), jnp.float32, smallest / len(pieces), top_value / len(pieces))
        gain = gain * jnp.repeat(jnp.exp(steps), extent[dim] // blocks).reshape((-1,) + (1,) * (len(extent) - 1 - dim))
    return gain


def deal_out(own_key, own, number, rows, number_of, top, limit, slope):
    sequence = jax.random.permutation(own_key, number_of)
    packed, usual = shares(number_of, rows * top, limit, slope, True), shares(number_of, rows * top, limit, slope, False)
    places = jnp.arange(number_of)

    def named(lengths, rotation):
        used = int((lengths > 0).sum())
        fixed = max(1, used // 4)
        passed = fixed + (places - fixed + rotation * (used - fixed)) % max(1, number_of - fixed)
        return jnp.zeros((number_of,), jnp.int32).at[sequence[jnp.where(places < fixed, places, passed)]].set(jnp.asarray(lengths, jnp.int32))

    lengths = jnp.where(number % 4 == 0, named(packed, number // 4), named(usual, number - number // 4 - 1))
    mixed = jax.random.permutation(jax.random.fold_in(own, 3), number_of)
    donor, receiver = mixed[0:number_of // 2 * 2:2], mixed[1:number_of // 2 * 2:2]
    margin = jnp.minimum(lengths[donor] - 1, limit - lengths[receiver]) // 2
    margin = jnp.where((donor == sequence[0]) | (receiver == sequence[0]) | (lengths[receiver] == 0), 0, jnp.maximum(margin, 0))
    passed = jax.random.randint(jax.random.fold_in(own, 4), (number_of // 2,), 0, 1 << 20) % (margin + 1)
    lengths = lengths.at[donor].add(-passed).at[receiver].add(passed)
    members = jnp.searchsorted(jnp.cumsum(lengths), jnp.arange(rows * top), side="right").astype(jnp.int32)
    grid = members.reshape(top, rows).T
    grid = grid[jax.random.permutation(jax.random.fold_in(own, 1), rows)]
    rotation = jax.random.randint(jax.random.fold_in(own, 2), (rows, 1), 0, top)
    return jnp.take_along_axis(grid, (jnp.arange(top)[None, :] + rotation) % top, axis=1)


def shares(count, total, reach, slope, full):
    weights = [(1 << 20) // math.isqrt(rank ** slope) + 1 for rank in range(1, count + 1)]
    largest = reach if full else min(reach, max(-(-total // count), total * weights[0] // sum(weights)))
    least = 1 if total - largest >= count - 1 else 0
    counts, spare = [largest] + [least] * (count - 1), total - largest - least * (count - 1)
    while spare > 0:
        free = [i for i in range(1, count) if counts[i] < largest] or [i for i in range(1, count) if counts[i] < reach]
        whole, remaining = sum([weights[i] for i in free]), spare
        for i in free:
            more = min(reach - counts[i], max(1, remaining * weights[i] // whole), spare)
            counts[i] = counts[i] + more
            spare = spare - more
    return np.array(counts)


def scatter_about(stream_key, shape, deviation, reach, cuts=(), dtype=jnp.bfloat16):
    gain = block_levels(stream_key, shape, cuts, -0.22, 0.18) if cuts else 1.0
    array = jax.random.normal(stream_key, shape, jnp.float32) * deviation * gain
    return jnp.minimum(jnp.maximum(array, -reach), reach).astype(dtype)


def setup_inputs(seed: int = 0) -> dict:
    seeds = jax.random.split(jax.random.key(seed), 15)
    stored = draw_stored(jax.random.fold_in(seeds[14], 71), 0)
    depth_weights = jnp.clip(jax.random.uniform(seeds[1], (DEPTH,), jnp.float32, 0.2, 1.0), 0.2, 1.0)
    attn_gain = jnp.clip(1.0 + 0.1 * jax.random.normal(seeds[2], (D,), jnp.float32), 0.5, 1.5)
    qkv_proj = scatter_about(seeds[3], (D, 3, HEADS, DH), D ** -0.5, 0.125, ((2, 4),))
    q_gain = jnp.clip(jnp.exp(math.log(2.5) - 0.916290732 * jax.random.uniform(seeds[4], (HEADS, DH), jnp.float32) ** block_levels(seeds[4], (HEADS, DH), ((0, 4),), -0.2, 0.2)), 1.0, 2.5)
    k_gain = jnp.clip(jnp.exp(math.log(2.5) - 0.916290732 * jax.random.uniform(seeds[5], (HEADS, DH), jnp.float32) ** block_levels(seeds[5], (HEADS, DH), ((0, 4),), -0.2, 0.2)), 1.0, 2.5)
    out_proj = scatter_about(seeds[6], (HEADS * DH, D), DH ** -0.5, 0.5, ((0, 4),))
    moe_gain = jnp.clip(1.0 + 0.1 * jax.random.normal(seeds[7], (D,), jnp.float32), 0.5, 1.5)
    router = scatter_about(seeds[8], (D, EXPERTS), D ** -0.5, 0.125)
    gate_proj = scatter_about(seeds[9], (D, EXPERTS * FF), D ** -0.5, 0.125, ((1, 32),))
    up_proj = scatter_about(seeds[10], (D, EXPERTS * FF), D ** -0.5, 0.125, ((1, 32),))
    down_proj = scatter_about(seeds[11], (EXPERTS * FF, D), FF ** -0.5, 0.15625, ((0, 32),))
    expert_ids_keys = jax.random.split(jax.random.fold_in(seeds[12], 1), SEQ // TOK)
    expert_ids_turns = jax.random.permutation(jax.random.fold_in(seeds[12], 3), SEQ // TOK)
    expert_ids = jax.vmap(lambda own, number: deal_out(jax.random.fold_in(seeds[12], 2), own, number, TOK, EXPERTS, TOPK, CAP, 2))(expert_ids_keys, expert_ids_turns).reshape((SEQ, TOPK))
    block_pattern = draw_block_pattern(jax.random.fold_in(seeds[14], 71), 0)
    return {"stored": stored, "depth_weights": depth_weights, "attn_gain": attn_gain, "qkv_proj": qkv_proj, "q_gain": q_gain, "k_gain": k_gain, "out_proj": out_proj, "moe_gain": moe_gain, "router": router, "gate_proj": gate_proj, "up_proj": up_proj, "down_proj": down_proj, "expert_ids": expert_ids, "block_pattern": block_pattern}


EPSILON = 1e-06

def rms_scale(values, gain_vec):
    mean_sq = lax.optimization_barrier(jnp.mean(values * values, axis=-1, keepdims=True))
    return values * lax.rsqrt(mean_sq + EPSILON) * gain_vec

def attend_blocks(q_blocks, key_blocks, value_blocks, pattern_rows, block_ids):
    listed = pattern_rows >= 0
    safe_ids = jnp.maximum(pattern_rows, 0)
    key_sel = jnp.take(key_blocks, safe_ids, axis=0)
    value_sel = jnp.take(value_blocks, safe_ids, axis=0)
    score_scale = q_blocks.shape[-1] ** (-0.5)
    scores = jnp.einsum('nid,nkjd->nikj', q_blocks.astype(jnp.float32), key_sel.astype(jnp.float32)) * score_scale
    diagonal = pattern_rows == block_ids[:, None]
    row_pos = lax.broadcasted_iota(jnp.int32, scores.shape, 1)
    col_pos = lax.broadcasted_iota(jnp.int32, scores.shape, 3)
    visible = listed[:, None, :, None] & (~diagonal[:, None, :, None] | (col_pos <= row_pos))
    weights = jnp.where(visible, jnp.exp(scores), jnp.float32(0.0))
    totals = lax.optimization_barrier(jnp.sum(weights, axis=(2, 3)))
    rounded = weights.astype(jnp.bfloat16).astype(jnp.float32)
    summed = jnp.einsum('nikj,nkjd->nid', rounded, value_sel.astype(jnp.float32))
    return (summed / totals[..., None]).astype(jnp.bfloat16)

def reference(stored, depth_weights, attn_gain, qkv_proj, q_gain, k_gain, out_proj, moe_gain, router, gate_proj, up_proj, down_proj, expert_ids, block_pattern):
    blended = depth_weights[0] * stored[0].astype(jnp.float32)
    for depth_step in range(1, DEPTH):
        blended = blended + depth_weights[depth_step] * stored[depth_step].astype(jnp.float32)
    inputs = blended.astype(jnp.bfloat16)
    normed = rms_scale(inputs.astype(jnp.float32), attn_gain).astype(jnp.bfloat16)
    projected = jnp.dot(normed, qkv_proj.reshape(D, 3 * HEADS * DH), preferred_element_type=jnp.float32)
    projected = projected.reshape(SEQ, 3, HEADS, DH)
    queries = rms_scale(projected[:, 0], q_gain).astype(jnp.bfloat16)
    key_heads = rms_scale(projected[:, 1], k_gain).astype(jnp.bfloat16)
    value_heads = projected[:, 2].astype(jnp.bfloat16)
    q_all = jnp.transpose(queries, (1, 0, 2)).reshape(HEADS, NB, BLK, DH)
    k_all = jnp.transpose(key_heads, (1, 0, 2)).reshape(HEADS, NB, BLK, DH)
    v_all = jnp.transpose(value_heads, (1, 0, 2)).reshape(HEADS, NB, BLK, DH)
    block_ids = jnp.arange(NB).astype(jnp.int32)

    def attend_head(operands):
        q_one, k_one, v_one, pattern_one = operands
        return attend_blocks(q_one, k_one, v_one, pattern_one, block_ids)
    attended = lax.map(attend_head, (q_all, k_all, v_all, block_pattern))
    attended = jnp.transpose(attended.reshape(HEADS, SEQ, DH), (1, 0, 2)).reshape(SEQ, HEADS * DH)
    attn_proj = jnp.dot(attended, out_proj, preferred_element_type=jnp.float32)
    residual = (inputs.astype(jnp.float32) + attn_proj).astype(jnp.bfloat16)
    moe_in = rms_scale(residual.astype(jnp.float32), moe_gain).astype(jnp.bfloat16)
    logits = jnp.dot(moe_in, router, preferred_element_type=jnp.float32)
    gate_vals = jax.nn.sigmoid(jnp.take_along_axis(logits, expert_ids, axis=1))
    flat_ids = expert_ids.reshape(-1)
    flat_gates = gate_vals.reshape(-1)
    most_rows = N_CTX * N_EXP * CAP

    def add_expert(expert_index, accum):
        matches = flat_ids == expert_index
        match_count = jnp.sum(matches.astype(jnp.int32))
        positions = jnp.nonzero(matches, size=most_rows, fill_value=0)[0].astype(jnp.int32)
        filled = jnp.arange(most_rows).astype(jnp.int32) < match_count
        token_ids = positions // TOPK
        row_vals = jnp.take(moe_in, token_ids, axis=0)
        w_gate = lax.dynamic_slice_in_dim(gate_proj, expert_index * FF, FF, 1)
        w_up = lax.dynamic_slice_in_dim(up_proj, expert_index * FF, FF, 1)
        w_down = lax.dynamic_slice_in_dim(down_proj, expert_index * FF, FF, 0)
        gate_act = jnp.dot(row_vals, w_gate, preferred_element_type=jnp.float32)
        up_act = jnp.dot(row_vals, w_up, preferred_element_type=jnp.float32)
        hidden = (jax.nn.silu(gate_act) * up_act).astype(jnp.bfloat16)
        out_rows = jnp.dot(hidden, w_down, preferred_element_type=jnp.float32).astype(jnp.bfloat16)
        weight = jnp.where(filled, jnp.take(flat_gates, positions), jnp.float32(0.0))
        return accum.at[token_ids].add(weight[:, None] * out_rows.astype(jnp.float32))
    moe_total = lax.fori_loop(0, EXPERTS, add_expert, jnp.zeros((SEQ, D), jnp.float32))
    return (residual.astype(jnp.float32) + moe_total).astype(jnp.bfloat16)
```

```python
import jax
import jax.numpy as jnp
from jax import lax
from jax.experimental import pallas as pl
from jax.experimental.layout import Layout, with_layout_constraint
from jax.experimental.pallas import tpu as pltpu
from jax.sharding import Mesh
from jax.sharding import PartitionSpec as P

BLK = 64
EPSILON = 1e-06
F32 = jnp.float32
BF16 = jnp.bfloat16


def swap(value, axis, mask):
    if isinstance(axis, tuple):
        size = 1
        for name in axis:
            size *= lax.axis_size(name)
    else:
        size = lax.axis_size(axis)
    return lax.ppermute(value, axis, [(i, i ^ mask) for i in range(size)])


def shift(value, axis, by):
    size = lax.axis_size(axis)
    return lax.ppermute(value, axis, [(i, (i + by) % size) for i in range(size)])


def around(value, axis):
    size = lax.axis_size(axis)
    held = [value] + [None] * (size - 1)
    for step in range(1, size // 2 + 1):
        held[step] = shift(held[step - 1], axis, 1)
        if size - step > step:
            held[size - step] = shift(held[(size - step + 1) % size], axis, -1)
    return held


def pick(array, index):
    return lax.dynamic_index_in_dim(array, index, 0, keepdims=False)


def rms_scale(values, gain_vec):
    mean_sq = jnp.mean(values * values, axis=-1, keepdims=True)
    return values * lax.rsqrt(mean_sq + EPSILON) * gain_vec


def attend_kernel(at_ref, q_ref, kv_ref, seen_ref, out_ref):
    count, per_list = at_ref.shape
    head_dim = q_ref.shape[2]
    wide = per_list * BLK
    row_pos = lax.broadcasted_iota(jnp.int32, (BLK, wide), 0)
    col_pos = lax.broadcasted_iota(jnp.int32, (BLK, wide), 1)
    causal = (col_pos >= BLK) | (col_pos <= row_pos)

    def one(n):
        listed = jnp.concatenate([kv_ref[at_ref[n, j]] for j in range(per_list)], axis=0)
        scores = lax.dot_general(
            q_ref[n], listed[:, :head_dim], (((1,), (1,)), ((), ())), preferred_element_type=F32
        ) * (head_dim ** (-0.5))
        weights = jnp.where(causal & (seen_ref[n] > 0), jnp.exp(scores), F32(0.0))
        totals = jnp.sum(weights, axis=1, keepdims=True)
        summed = jnp.dot(weights.astype(BF16), listed[:, head_dim:], preferred_element_type=F32)
        out_ref[n] = (summed / totals).astype(BF16)

    together = 4 if count % 4 == 0 else 1

    def step(i, carry):
        for u in range(together):
            one(i * together + u)
        return carry

    lax.fori_loop(0, count // together, step, 0)


def attend(stored_at, q_blocks, kv_blocks, seen):
    whole = pl.BlockSpec(memory_space=pltpu.VMEM)
    n, width = stored_at.shape[0], stored_at.shape[1] * BLK
    head_dim = q_blocks.shape[2]
    return pl.pallas_call(
        attend_kernel,
        out_shape=jax.ShapeDtypeStruct(q_blocks.shape, BF16),
        in_specs=[pl.BlockSpec(memory_space=pltpu.SMEM), whole, whole, whole],
        out_specs=whole,
        compiler_params=pltpu.CompilerParams(vmem_limit_bytes=32 * 2**20),
        cost_estimate=pl.CostEstimate(
            flops=4 * n * BLK * width * head_dim,
            bytes_accessed=4 * kv_blocks.size,
            transcendentals=n * BLK * width,
        ),
    )(stored_at, q_blocks, kv_blocks, seen)


def expert_kernel(x_ref, g0, u0, d0, g1, u1, d1, out_ref, w_gate, w_up, w_down, hidden, partial, sems):
    copies = []
    for i, (src, dst) in enumerate(
        ((g0, w_gate.at[0]), (u0, w_up.at[0]), (d0, w_down.at[0]), (g1, w_gate.at[1]), (u1, w_up.at[1]), (d1, w_down.at[1]))
    ):
        copies.append(pltpu.make_async_copy(src, dst, sems.at[i]))
        copies[-1].start()
    across = (((1,), (1,)), ((), ()))
    count, feat = x_ref.shape
    tile = 256 if count % 256 == 0 else count
    wide = 512 if feat % 512 == 0 else feat
    for part in range(2):
        copies[3 * part].wait()
        copies[3 * part + 1].wait()

        @pl.loop(0, count // tile)
        def _(i):
            rows = pl.ds(pl.multiple_of(i * tile, tile), tile)
            gate_act = lax.dot_general(x_ref[rows, :], w_gate[part], across, preferred_element_type=F32)
            up_act = lax.dot_general(x_ref[rows, :], w_up[part], across, preferred_element_type=F32)
            hidden[rows, :] = (gate_act / (1.0 + jnp.exp(-gate_act)) * up_act).astype(BF16)

        copies[3 * part + 2].wait()

        @pl.loop(0, count // tile)
        def _(i):
            rows = pl.ds(pl.multiple_of(i * tile, tile), tile)
            for start in range(0, feat, wide):
                cols = slice(start, start + wide)
                term = jnp.dot(hidden[rows, :], w_down[part, :, cols], preferred_element_type=F32)
                if part == 0:
                    partial[rows, cols] = term
                else:
                    out_ref[rows, cols] = (partial[rows, cols] + term).astype(BF16)


def expert(rows, *weights):
    count, feat = rows.shape
    units = weights[0].shape[0]
    whole = pl.BlockSpec(memory_space=pltpu.VMEM)
    return pl.pallas_call(
        expert_kernel,
        out_shape=jax.ShapeDtypeStruct((count, feat), BF16),
        in_specs=[whole] + [pl.BlockSpec(memory_space=pl.ANY)] * 6,
        out_specs=whole,
        scratch_shapes=[
            pltpu.VMEM((2, units, feat), BF16),
            pltpu.VMEM((2, units, feat), BF16),
            pltpu.VMEM((2, units, feat), BF16),
            pltpu.VMEM((count, units), BF16),
            pltpu.VMEM((count, feat), F32),
            pltpu.SemaphoreType.DMA((6,)),
        ],
        compiler_params=pltpu.CompilerParams(vmem_limit_bytes=44 * 2**20),
        cost_estimate=pl.CostEstimate(
            flops=12 * count * feat * units,
            bytes_accessed=12 * feat * units + 4 * count * feat,
            transcendentals=2 * count * units,
        ),
    )(rows, *weights)


def body(
    stored,
    depth_weights,
    attn_gain,
    qkv_proj,
    q_gain,
    k_gain,
    out_proj,
    moe_gain,
    router,
    gate_proj,
    up_proj,
    down_proj,
    expert_ids,
    block_pattern,
):
    nz, nx, ne, ns = (lax.axis_size(name) for name in ("z", "x", "ep", "s"))
    iz, ix, ie, js = (lax.axis_index(name) for name in ("z", "x", "ep", "s"))
    depth_count, shard_len, feat = stored.shape
    head_dim = qkv_proj.shape[3]
    heads = qkv_proj.shape[2]
    tok = shard_len // (ne * ns)

    gate_proj, up_proj = gate_proj.T, up_proj.T
    gate_other = swap(gate_proj, "s", 1)
    up_other = swap(up_proj, "s", 1)
    down_other = swap(down_proj, "s", 1)
    ids = around(expert_ids, "z")

    blended = depth_weights[0] * stored[0].astype(F32)
    for depth_step in range(1, depth_count):
        blended = blended + depth_weights[depth_step] * stored[depth_step].astype(F32)
    inputs = blended.astype(BF16)
    normed = rms_scale(inputs.astype(F32), attn_gain).astype(BF16)
    projected = jnp.einsum("td,dche->chte", normed, qkv_proj, preferred_element_type=F32)
    projected = with_layout_constraint(projected, Layout(major_to_minor=(0, 1, 2, 3)))
    queries = rms_scale(projected[0], q_gain[:, None, :]).astype(BF16)
    keys = rms_scale(projected[1], k_gain[:, None, :]).astype(BF16)
    values = projected[2].astype(BF16)

    kv = jnp.concatenate([keys, values], axis=2)
    q_parts, kv_parts = [], []
    for m in range(nz):
        q_one, kv_one = pick(queries, iz ^ m), pick(kv, iz ^ m)
        if m:
            kv_one = swap(kv_one, "z", m)
            q_one = swap(q_one, "z", m)
        q_parts.append(q_one)
        pieces = [kv_one]
        step = 1
        while step < nx:
            pieces = pieces + [swap(piece, "x", step) for piece in pieces]
            step *= 2
        kv_parts.extend(pieces)
    kv_all = jnp.concatenate(kv_parts, axis=0)
    per_shard = shard_len // BLK
    kv_blocks = kv_all.reshape(-1, BLK, 2 * head_dim)
    own_head = (ie * ns + js) * heads + iz
    pattern = pick(block_pattern, own_head)
    pattern = pick(jnp.moveaxis(pattern.reshape(nz, nx, per_shard, -1), 1, 0), ix)
    pattern_rows = jnp.concatenate([pick(pattern, iz ^ m) for m in range(nz)], axis=0)
    safe_ids = jnp.maximum(pattern_rows, 0)
    shard = safe_ids // per_shard
    stored_at = (((shard // nx) ^ iz) * nx + ((shard % nx) ^ ix)) * per_shard + safe_ids % per_shard
    q_blocks = jnp.concatenate(q_parts, axis=0).reshape(-1, BLK, head_dim)
    seen = jnp.repeat((pattern_rows >= 0).astype(jnp.int32), BLK, axis=1)[:, None, :]
    attended = attend(stored_at, q_blocks, kv_blocks, seen).reshape(nz, shard_len, head_dim)

    out_weight = out_proj.reshape(heads, head_dim, feat)
    back = [attended[0]] + [swap(attended[m], "z", m) for m in range(1, nz)]
    weight_rows = jnp.concatenate([pick(out_weight, iz ^ m) for m in range(nz)], axis=0)
    attn_part = jnp.dot(jnp.concatenate(back, axis=1), weight_rows, preferred_element_type=F32)

    parts = attn_part.reshape(ne, ns, tok, feat)
    keep = lax.dynamic_index_in_dim(parts, js, 1, keepdims=False)
    give = lax.dynamic_index_in_dim(parts, js ^ 1, 1, keepdims=False).astype(BF16)
    pair_sum = keep + swap(give, "s", 1).astype(F32)
    attn_sum = pick(pair_sum, ie)
    for m in range(1, ne):
        attn_sum = attn_sum + swap(pick(pair_sum, ie ^ m).astype(BF16), "ep", m).astype(F32)

    own_rows = lax.dynamic_slice_in_dim(inputs, (ie * ns + js) * tok, tok, 0)
    residual = (own_rows.astype(F32) + attn_sum).astype(BF16)
    moe_in = rms_scale(residual.astype(F32), moe_gain).astype(BF16)

    plane = nx * ne
    me = ix * ne + ie
    experts = nz * plane
    capacity = 8 * tok // experts
    plane_ids = iz * plane + (jnp.arange(plane, dtype=jnp.int32) ^ me)
    before = (
        lax.broadcasted_iota(jnp.int32, (tok, tok), 0) > lax.broadcasted_iota(jnp.int32, (tok, tok), 1)
    ).astype(BF16)
    expert_cols = (jnp.arange(experts, dtype=jnp.int32)[:, None] == plane_ids[None, :]).astype(F32)

    def routing(ids_k):
        named = jnp.any(ids_k[:, :, None] == plane_ids[None, None, :], axis=1)
        order = jnp.dot(before, named.astype(BF16), preferred_element_type=F32)
        slots = jnp.where(named, order, F32(-1.0)).T
        steps = lax.broadcasted_iota(jnp.int32, (1, capacity, 1), 1).astype(F32)
        return (slots[:, None, :] == steps).reshape(plane * capacity, tok)

    places = [routing(ids_k) for ids_k in ids]
    chunks = around(moe_in, "z")

    def exchange(rows):
        rows = rows.reshape(plane, -1, feat)
        got = [rows[0]] + [swap(rows[m], ("x", "ep"), m) for m in range(1, plane)]
        return jnp.concatenate(got, axis=0)

    weights = (gate_proj, up_proj, down_proj, gate_other, up_other, down_other)

    def processed(group):
        sent = [
            jnp.dot(places[k].astype(BF16), chunks[k], preferred_element_type=F32)
            .astype(BF16)
            .reshape(plane, capacity, feat)
            for k in group
        ]
        done = exchange(expert(exchange(jnp.concatenate(sent, axis=1)), *weights))
        done = done.reshape(plane, len(group), capacity, feat)
        return {k: done[:, i].reshape(plane * capacity, feat) for i, k in enumerate(group)}

    def contribution(k, done):
        logits = jnp.dot(chunks[k], router, preferred_element_type=F32)
        gates = jax.nn.sigmoid(jnp.dot(logits, expert_cols, precision=lax.Precision.HIGHEST))
        gates = jnp.repeat(gates.T, capacity, axis=0)
        weight = jnp.where(places[k], gates, F32(0.0))
        high = weight.astype(BF16)
        low = (weight - high.astype(F32)).astype(BF16)
        over_rows = (((0,), (0,)), ((), ()))
        return lax.dot_general(high, done, over_rows, preferred_element_type=F32) + lax.dot_general(
            low, done, over_rows, preferred_element_type=F32
        )

    terms = [None] * nz
    half = nz // 2
    for group in (range(half), range(half, nz)):
        for k, done in processed(list(group)).items():
            terms[k] = contribution(k, done)

    total = terms[0]
    for indices, by in ((range(half, 0, -1), -1), (range(half + 1, nz), 1)):
        moving = None
        for k in indices:
            moving = terms[k] if moving is None else terms[k] + moving
            moving = shift(moving.astype(BF16), "z", by).astype(F32)
        if moving is not None:
            total = total + moving
    return (residual.astype(F32) + total).astype(BF16)


def solution(mesh):
    n_ctx, n_exp = mesh.shape["ctx"], mesh.shape["exp"]

    def fn(*args):
        far = args[3].shape[2] // n_exp
        split = Mesh(
            mesh.devices.reshape(far, n_ctx // far, n_exp // 2, 2), ("z", "x", "ep", "s")
        )
        ctx, exp, both = ("z", "x"), ("ep", "s"), ("z", "x", "ep", "s")
        return jax.shard_map(
            body,
            mesh=split,
            in_specs=(
                P(None, ctx, None),
                P(),
                P(),
                P(None, None, exp, None),
                P(exp, None),
                P(exp, None),
                P(exp, None),
                P(),
                P(),
                P(None, both),
                P(None, both),
                P(both, None),
                P(both, None),
                P(),
            ),
            out_specs=P(both, None),
            check_vma=False,
        )(*args)

    return fn
```
